32 devices in a mesh: az: 8 (over z, x), ht: 4 (over y, core).
Axes of the slice: x: 2, y: 2, z: 4, core: 2. Of those that a mesh axis runs over, the one named last changes fastest.
Arguments:
- object_field: bfloat16 [256, 3, 2, 4096], P('ht', None, None, 'az'), may hold values from -6 to 6
- propagator: bfloat16 [3, 2, 256, 256], replicated, may hold values from -0.25 to 0.25
- kernel_taps: float32 [3, 2, 129], replicated, may hold values from -0.5 to 0.5
- band_reach: int32 [3], replicated, may hold values from 16 to 64, as said below
- sector_offset: int32 [8], replicated, may hold values from 0 to 511, as said below
- sector_width: int32 [8], replicated, may hold values from 768 to 1536
- target_index: int32 [8], replicated, may hold values from 0 to 3
- target_maps: float32 [4, 256, 3, 256], P(None, 'ht'), may hold values from 0 to 3
Outputs:
- object_grad: float32 [256, 3, 2, 4096], P('ht', None, None, 'az')
The draws below stay inside these ranges and needn't reach their ends.
Inputs may be any that keep to these rules, and one draw needn't show every extreme that they name: One wavelength has band_reach 64, another 64 // 4. Sector s's window begins at azimuth s * 512 + sector_offset[s] and wraps around the cylinder.
All inputs are finite; a program needn't handle non-finite values.
Results may differ from the reference program's by a relative error of at most 0.0095.
Values may be sent and summed in bfloat16 or wider, within the bound.
A program may use at most 64 MiB of HBM per device.

```python
import math
import jax
import jax.numpy as jnp
from jax import lax

HEIGHT = 256
WAVES = 3
FREQS = 256
REACH = 64
PATTERNS = 4
AZ_DEV = 512
AZIMUTH = 4096
SECTORS = 8


def sector_pair(key):
    inner = jax.random.fold_in(key, 11)
    first, second, third = jax.random.split(inner, 3)
    offsets = jax.random.randint(first, (SECTORS,), 0, AZ_DEV)
    widths = jax.random.randint(second, (SECTORS,), 3 * AZ_DEV // 2, 3 * AZ_DEV + 1)
    order = jax.random.permutation(third, SECTORS)
    offsets = offsets.at[order[0]].set(AZ_DEV - 1).at[order[1]].set(0)
    widths = widths.at[order[0]].set(3 * AZ_DEV).at[order[1]].set(3 * AZ_DEV // 2)
    return (offsets.astype(jnp.int32), widths.astype(jnp.int32))


def draw_sector_offset(key, part):
    return sector_pair(key)[0]


def draw_sector_width(key, part):
    return sector_pair(key)[1]


def draw_band_reach(key, part):
    inner = jax.random.fold_in(key, 23)
    first, second = jax.random.split(inner)
    values = jax.random.randint(first, (WAVES,), REACH // 4, REACH + 1)
    order = jax.random.permutation(second, WAVES)
    values = values.at[order[0]].set(REACH).at[order[1]].set(REACH // 4)
    return values.astype(jnp.int32)


def touch_ends(drawn, key, least, high):
    spot = [jax.random.randint(jax.random.fold_in(key, axis), (), 0, length) for axis, length in enumerate(drawn.shape)]
    widest = drawn.shape.index(max(drawn.shape))
    neighbour = spot[:widest] + [(spot[widest] + 1) % drawn.shape[widest]] + spot[widest + 1:]
    return drawn.at[tuple(spot)].set(least).at[tuple(neighbour)].set(high)


def shard_levels(rng, shape, cuts, smallest, top_value):
    level = 1.0
    for position, shards_of in cuts:
        draws = jax.random.uniform(jax.random.fold_in(jax.random.fold_in(rng, 6), position), (shards_of,), jnp.float32, smallest / len(cuts), top_value / len(cuts))
        level = level * jnp.repeat(jnp.exp(draws), shape[position] // shards_of).reshape((-1,) + (1,) * (len(shape) - 1 - position))
    return level


def gaussian(own_key, shape, spread, reach, shards=(), held_as=jnp.bfloat16):
    array = spread * jax.random.normal(own_key, shape, jnp.float32)
    if shards:
        array = array * shard_levels(own_key, shape, shards, -0.22, 0.18)
    return jnp.clip(array, -reach, reach).astype(held_as)


def setup_inputs(seed: int = 0) -> dict:
    arg_keys = jax.random.split(jax.random.key(seed), 9)
    object_field = gaussian(arg_keys[0], (HEIGHT, WAVES, 2, AZIMUTH), 1.0, 6.0, ((0, 4), (3, 8)))
    propagator = gaussian(arg_keys[1], (WAVES, 2, HEIGHT, HEIGHT), (2 * HEIGHT) ** -0.5, 0.25)
    kernel_taps = gaussian(arg_keys[2], (WAVES, 2, 2 * REACH + 1), (2 * REACH + 2) ** -0.5, 0.5, (), jnp.float32)
    band_reach = draw_band_reach(jax.random.fold_in(arg_keys[8], 71), 0)
    sector_offset = draw_sector_offset(jax.random.fold_in(arg_keys[8], 71), 0)
    sector_width = draw_sector_width(jax.random.fold_in(arg_keys[8], 71), 0)
    target_index = touch_ends(jax.random.randint(arg_keys[6], (SECTORS,), 0, PATTERNS), jax.random.fold_in(arg_keys[6], 1), 0, PATTERNS - 1).astype(jnp.int32)
    target_maps = jnp.clip(3.0 * jax.random.uniform(arg_keys[7], (PATTERNS, HEIGHT, WAVES, FREQS), jnp.float32) ** shard_levels(arg_keys[7], (PATTERNS, HEIGHT, WAVES, FREQS), ((1, 4),), -0.2, 0.2), 0.0, 3.0)
    return dict(object_field=object_field, propagator=propagator, kernel_taps=kernel_taps, band_reach=band_reach, sector_offset=sector_offset, sector_width=sector_width, target_index=target_index, target_maps=target_maps)


HIGHEST = lax.Precision.HIGHEST

def height_block(propagator):
    real_part = propagator[:, 0]
    imag_part = propagator[:, 1]
    upper = jnp.stack([real_part, -imag_part], axis=2)
    lower = jnp.stack([imag_part, real_part], axis=2)
    return jnp.stack([upper, lower], axis=1)

def masked(kernel_taps, band_reach):
    distance = jnp.abs(jnp.arange(2 * REACH + 1, dtype=jnp.int32) - REACH)
    keep = distance[None, :] <= band_reach[:, None]
    return jnp.where(keep[:, None, :], kernel_taps, jnp.zeros_like(kernel_taps))

def toeplitz(real_taps, imag_taps):
    block_size = 2 * REACH
    period = 3 * block_size
    wave_count = real_taps.shape[0]

    def arrange(tap_values):
        padded = jnp.concatenate([tap_values, jnp.zeros((wave_count, period - block_size - 1), tap_values.dtype)], axis=1)
        tiled = jnp.tile(padded, (1, block_size))[:, :block_size * (period - 1)]
        return tiled.reshape(wave_count, block_size, period - 1)[:, :, :2 * block_size]
    real_lay = arrange(real_taps)
    imag_lay = arrange(imag_taps)
    upper = jnp.stack([real_lay, imag_lay], axis=1)
    lower = jnp.stack([-imag_lay, real_lay], axis=1)
    return jnp.stack([upper, lower], axis=1).astype(jnp.bfloat16)

def convolve(extended, coupling):
    row_count, wave_count, part_count, full_length = extended.shape
    block_size = 2 * REACH
    block_count = full_length // block_size - 1
    shaped = extended.reshape(row_count, wave_count, part_count, block_count + 1, block_size)
    windows = jnp.concatenate([shaped[:, :, :, :-1], shaped[:, :, :, 1:]], axis=4)
    result = jnp.einsum('hwcbi,wcdji->hwdbj', windows.astype(jnp.float32), coupling.astype(jnp.float32), precision=HIGHEST)
    return result.reshape(row_count, wave_count, part_count, block_count * block_size)

def spectrum_table(offset, span_width, az_count):
    places = jnp.arange(4 * az_count, dtype=jnp.int32) - offset
    inside = (places >= 0) & (places < span_width)
    places = jnp.where(inside, places, 0)
    frequency = jnp.arange(FREQS, dtype=jnp.int32)
    phases = jnp.mod(places[:, None] * frequency[None, :], FREQS).astype(jnp.float32) * (2.0 * math.pi / FREQS)
    span_float = span_width.astype(jnp.float32)
    taper = 0.5 - 0.5 * jnp.cos((places.astype(jnp.float32) + 0.5) * (2.0 * math.pi) / span_float)
    taper = jnp.where(inside, taper, 0.0) / jnp.sqrt(span_float)
    cosine = taper[:, None] * jnp.cos(phases)
    sine = taper[:, None] * jnp.sin(phases)
    upper = jnp.stack([cosine, -sine], axis=1)
    lower = jnp.stack([sine, cosine], axis=1)
    return jnp.stack([upper, lower], axis=0).astype(jnp.bfloat16)

def view_slopes(window, spectra_table, target_plane):
    spectrum = jnp.einsum('hwcp,cpdk->hwdk', window.astype(jnp.float32), spectra_table.astype(jnp.float32), precision=HIGHEST)
    power = spectrum[:, :, 0] * spectrum[:, :, 0] + spectrum[:, :, 1] * spectrum[:, :, 1]
    misfit = power - target_plane
    slope = (2.0 * misfit[:, :, None, :] * spectrum).astype(jnp.bfloat16)
    back = jnp.einsum('hwdk,cpdk->hwcp', slope.astype(jnp.float32), spectra_table.astype(jnp.float32), precision=HIGHEST)
    return back.astype(jnp.bfloat16)

def reference(object_field, propagator, kernel_taps, band_reach, sector_offset, sector_width, target_index, target_maps):
    coupling = height_block(propagator).astype(jnp.float32)
    height_field = jnp.einsum('wdhcg,gwca->hwda', coupling, object_field.astype(jnp.float32), precision=HIGHEST).astype(jnp.bfloat16)
    masked_taps = masked(kernel_taps, band_reach)
    forward = toeplitz(masked_taps[:, 0], masked_taps[:, 1])
    backward = toeplitz(masked_taps[:, 0, ::-1], -masked_taps[:, 1, ::-1])

    def by_groups(values, matrix):
        shaped = values.reshape(HEIGHT // 32, 32, WAVES, 2, AZIMUTH)

        def single(group_rows):
            extended = jnp.concatenate([group_rows[..., AZIMUTH - REACH:], group_rows, group_rows[..., :REACH]], axis=3)
            return convolve(extended, matrix).astype(jnp.bfloat16)
        return lax.map(single, shaped).reshape(HEIGHT, WAVES, 2, AZIMUTH)
    hologram = by_groups(height_field, forward)
    wrapped = jnp.concatenate([hologram, hologram[..., :3 * AZ_DEV]], axis=3)

    def sector_step(summed, index):
        spectra_table = spectrum_table(sector_offset[index], sector_width[index], AZ_DEV)
        anchor = index * AZ_DEV
        window = lax.dynamic_slice_in_dim(wrapped, anchor, 4 * AZ_DEV, 3)
        slopes = view_slopes(window, spectra_table, target_maps[target_index[index]])
        current = lax.dynamic_slice_in_dim(summed, anchor, 4 * AZ_DEV, 3)
        summed = lax.dynamic_update_slice_in_dim(summed, current + slopes.astype(jnp.float32), anchor, 3)
        return (summed, None)
    initial = jnp.zeros((HEIGHT, WAVES, 2, AZIMUTH + 3 * AZ_DEV), jnp.float32)
    summed, unused = lax.scan(sector_step, initial, jnp.arange(SECTORS, dtype=jnp.int32))
    folded = summed[..., :AZIMUTH].at[..., :3 * AZ_DEV].add(summed[..., AZIMUTH:])
    hologram_grad = folded.astype(jnp.bfloat16)
    field_grad = by_groups(hologram_grad, backward)
    return jnp.einsum('wdhcg,hwda->gwca', coupling, field_grad.astype(jnp.float32), precision=HIGHEST)
```

```python
import math

import jax
import jax.numpy as jnp
import ml_dtypes
import numpy as np
from jax import lax
from jax.sharding import PartitionSpec as P

FREQS = 256
REACH = 64


def with_halo(x, sides, width):
    for axis, dim in sides:
        size, length = (lax.axis_size(axis), x.shape[dim])
        up = [(i, (i + 1) % size) for i in range(size)]
        down = [(j, i) for i, j in up]
        last = lax.slice_in_dim(x, length - width, length, axis=dim)
        initial = lax.slice_in_dim(x, 0, width, axis=dim)
        before = lax.ppermute(last, axis, up)
        after = lax.ppermute(initial, axis, down)
        x = jnp.concatenate([before, x, after], axis=dim)
    return x


def from_behind(block, axis, distance):
    devices = range(lax.axis_size(axis))
    route = [((i - distance) % len(devices), i) for i in devices]
    return lax.ppermute(block, axis, route)


def height_block(propagator):
    real_part = propagator[:, 0]
    imag_part = propagator[:, 1]
    upper = jnp.stack([real_part, -imag_part], axis=2)
    lower = jnp.stack([imag_part, real_part], axis=2)
    return jnp.stack([upper, lower], axis=1)


def masked(kernel_taps, band_reach):
    distance = jnp.abs(jnp.arange(2 * REACH + 1, dtype=jnp.int32) - REACH)
    keep = distance[None, :] <= band_reach[:, None]
    return jnp.where(keep[:, None, :], kernel_taps, jnp.zeros_like(kernel_taps))


def toeplitz(real_taps, imag_taps):
    block_size = 2 * REACH
    period = 3 * block_size
    wave_count = real_taps.shape[0]

    def arrange(tap_values):
        padded = jnp.concatenate(
            [tap_values, jnp.zeros((wave_count, period - block_size - 1), tap_values.dtype)], axis=1
        )
        tiled = jnp.tile(padded, (1, block_size))[:, : block_size * (period - 1)]
        return tiled.reshape(wave_count, block_size, period - 1)[:, :, : 2 * block_size]

    real_lay = arrange(real_taps)
    imag_lay = arrange(imag_taps)
    upper = jnp.stack([real_lay, imag_lay], axis=1)
    lower = jnp.stack([-imag_lay, real_lay], axis=1)
    return jnp.stack([upper, lower], axis=1).astype(jnp.bfloat16)


def convolve(extended, coupling):
    row_count, wave_count, part_count, full_length = extended.shape
    block_size = 2 * REACH
    block_count = full_length // block_size - 1
    shaped = extended.reshape(row_count, wave_count, part_count, block_count + 1, block_size)
    windows = jnp.concatenate([shaped[:, :, :, :-1], shaped[:, :, :, 1:]], axis=4)
    result = jnp.einsum("hwcbi,wcdji->hwdbj", windows, coupling, preferred_element_type=jnp.float32)
    return result.reshape(row_count, wave_count, part_count, block_count * block_size)


def taper_row(offset, span_width, length):
    places = jnp.arange(length, dtype=jnp.int32) - offset
    inside = (places >= 0) & (places < span_width)
    places = jnp.where(inside, places, 0)
    span_float = span_width.astype(jnp.float32)
    taper = 0.5 - 0.5 * jnp.cos((places.astype(jnp.float32) + 0.5) * (2.0 * math.pi) / span_float)
    return jnp.where(inside, taper, 0.0) / jnp.sqrt(span_float)


def dft_pair():
    index = np.arange(FREQS)
    phases = (index[:, None] * index[None, :] % FREQS) * (2.0 * np.pi / FREQS)
    cosine, sine = np.cos(phases), np.sin(phases)
    table = np.stack([np.stack([cosine, -sine], axis=1), np.stack([sine, cosine], axis=1)], axis=0)
    return table.astype(ml_dtypes.bfloat16)


def on_device(
    object_field,
    propagator,
    kernel_taps,
    band_reach,
    sector_offset,
    sector_width,
    target_index,
    target_maps,
):
    row_count, wave_count, part_count, az_count = object_field.shape
    loop_size = lax.axis_size("az")
    first_row = lax.axis_index("ht") * row_count
    coupling = height_block(propagator)
    own_rows = lax.dynamic_slice_in_dim(coupling, first_row, row_count, 2)
    zero_field = jnp.zeros((row_count, wave_count, part_count, az_count), jnp.float32)
    columns = own_rows
    height_field = jnp.einsum(
        "wdhcg,gwca->hwda",
        columns,
        lax.all_gather(object_field, "ht", axis=0, tiled=True),
        preferred_element_type=jnp.float32,
    ).astype(jnp.bfloat16)
    masked_taps = masked(kernel_taps, band_reach)
    forward = toeplitz(masked_taps[:, 0], masked_taps[:, 1])
    backward = toeplitz(masked_taps[:, 0, ::-1], -masked_taps[:, 1, ::-1])
    extended = with_halo(height_field, (("az", 3),), REACH)
    hologram = convolve(extended, forward).astype(jnp.bfloat16)
    here = lax.axis_index("az")
    rows, waves, parts, length = hologram.shape
    tapers = []
    for back in range(4):
        sector = jnp.mod(here - back, loop_size)
        row = taper_row(sector_offset[sector], sector_width[sector], 4 * length)
        tapers.append(row[back * length : (back + 1) * length])
    wide = hologram.astype(jnp.float32)
    folded = jnp.zeros((rows, waves, parts, FREQS), jnp.float32)
    for back in range(4):
        part = (wide * tapers[back]).reshape(rows, waves, parts, length // FREQS, FREQS)
        part = jnp.sum(part, axis=3)
        if back:
            part = from_behind(part.astype(jnp.bfloat16), "az", -back).astype(jnp.float32)
        folded = folded + part
    table = jnp.asarray(dft_pair())
    pattern = target_index[here]
    target_plane = lax.dynamic_index_in_dim(target_maps, pattern, 0, False)
    spectrum = jnp.einsum(
        "hwcp,cpdk->hwdk", folded.astype(jnp.bfloat16), table, preferred_element_type=jnp.float32
    )
    power = spectrum[:, :, 0] * spectrum[:, :, 0] + spectrum[:, :, 1] * spectrum[:, :, 1]
    misfit = power - target_plane
    slope = (2.0 * misfit[:, :, None, :] * spectrum).astype(jnp.bfloat16)
    returned = jnp.einsum("hwdk,cpdk->hwcp", slope, table, preferred_element_type=jnp.float32)
    returned = returned.astype(jnp.bfloat16)
    summed = zero_field
    for back in range(4):
        part = from_behind(returned, "az", back) if back else returned
        part = jnp.tile(part.astype(jnp.float32), (1, 1, 1, length // FREQS))
        summed = summed + part * tapers[back]
    hologram_grad = summed.astype(jnp.bfloat16)
    grad_extended = with_halo(hologram_grad, (("az", 3),), REACH)
    field_grad = convolve(grad_extended, backward).astype(jnp.bfloat16)
    columns = own_rows
    return lax.psum_scatter(
        jnp.einsum(
            "wdhcg,hwda->gwca", columns, field_grad, preferred_element_type=jnp.float32
        ).astype(jnp.bfloat16),
        "ht",
        scatter_dimension=0,
        tiled=True,
    ).astype(jnp.float32)


def solution(mesh):
    in_specs = (P("ht", None, None, "az"), P(), P(), P(), P(), P(), P(), P(None, "ht", None, None))
    out_specs = P("ht", None, None, "az")
    return jax.shard_map(
        on_device, mesh=mesh, in_specs=in_specs, out_specs=out_specs, check_vma=False
    )
```

```python
import functools
import math

import jax
import jax.numpy as jnp
import ml_dtypes
import numpy as np
from jax import lax
from jax.experimental import pallas as pl
from jax.experimental.pallas import tpu as pltpu
from jax.sharding import PartitionSpec as P

FREQS = 256
REACH = 64
LANES = 128
SPAN = 4
MESH = pl.DeviceIdType.MESH


def masked(kernel_taps, band_reach):
    distance = jnp.abs(jnp.arange(2 * REACH + 1, dtype=jnp.int32) - REACH)
    keep = distance[None, :] <= band_reach[:, None]
    return jnp.where(keep[:, None, :], kernel_taps, jnp.zeros_like(kernel_taps))


def taper_row(offset, span_width, first, length):
    places = first + jnp.arange(length, dtype=jnp.int32) - offset
    inside = (places >= 0) & (places < span_width)
    places = jnp.where(inside, places, 0)
    span_float = span_width.astype(jnp.float32)
    taper = 0.5 - 0.5 * jnp.cos((places.astype(jnp.float32) + 0.5) * (2.0 * math.pi) / span_float)
    return jnp.where(inside, taper, 0.0) / jnp.sqrt(span_float)


def dft_table(quarters):
    index = np.arange(FREQS)
    phases = (index[:, None] * index[None, :] % FREQS) * (2.0 * np.pi / FREQS)
    cosine, sine = np.cos(phases), np.sin(phases)
    table = np.stack([np.stack([cosine, -sine], axis=1), np.stack([sine, cosine], axis=1)], axis=0)
    table = table.reshape(2, FREQS, 2, quarters, FREQS // quarters).transpose(0, 1, 3, 2, 4)
    return table.reshape(2 * FREQS, 2 * FREQS).astype(ml_dtypes.bfloat16)


def toeplitz_kernel(seq_ref, out_ref):
    for way in range(2):
        for wave in range(seq_ref.shape[1]):
            lay = []
            for part in range(2):
                row = seq_ref[way, wave, part : part + 1, :]
                spread = jnp.broadcast_to(row, (3 * LANES, 4 * LANES))
                turned = pltpu.roll(spread, 320, 1, stride=1, stride_axis=0)
                lay.append(turned[:, :LANES])
            upper = jnp.concatenate([lay[0], lay[1]], axis=1)
            lower = jnp.concatenate([-lay[1], lay[0]], axis=1)
            out_ref[way, wave] = jnp.concatenate([upper, lower], axis=0).astype(jnp.bfloat16)


def toeplitz_tables(kernel_taps, band_reach):
    taps = masked(kernel_taps, band_reach)
    turned = taps[:, :, ::-1]
    conj = taps * jnp.array([1.0, -1.0], jnp.float32)[None, :, None]
    seq = jnp.stack([turned, conj], axis=0)
    seq = jnp.pad(seq, ((0, 0), (0, 0), (0, 0), (0, 4 * LANES - seq.shape[3])))
    waves = taps.shape[0]
    return pl.pallas_call(
        toeplitz_kernel,
        out_shape=jax.ShapeDtypeStruct((2, waves, 6 * LANES, 2 * LANES), jnp.bfloat16),
        in_specs=[pl.BlockSpec(memory_space=pltpu.VMEM)],
        out_specs=pl.BlockSpec(memory_space=pltpu.VMEM),
    )(seq)


def windows(own, left, right):
    stack = []
    for block in range(4):
        row = []
        for part in range(2):
            for near in (block - 1, block, block + 1):
                if near < 0:
                    row.append(left[:, part * LANES : (part + 1) * LANES])
                elif near > 3:
                    row.append(right[:, part * LANES : (part + 1) * LANES])
                else:
                    start = (part * 4 + near) * LANES
                    row.append(own[:, start : start + LANES])
        stack.append(jnp.concatenate(row, axis=1))
    return jnp.concatenate(stack, axis=0)


def fused_kernel(
    az_size, ht_size, x_ref, toep_ref, taper_ref, dft_ref, idft_ref, prop_ref, propt_ref, target_ref,
    out_ref, edges, halo, send_u, recv_u, recv_t, send_g, recv_g, grad, gedges, ghalo,
    sem_hs, sem_hr, sem_us, sem_ur, sem_ts, sem_tr, sem_gs, sem_gr, sem_bs, sem_br,
):
    a = lax.axis_index("az")
    r = lax.axis_index("ht")
    waves, rows, _ = x_ref.shape
    height = rows * ht_size

    def az(distance):
        return lax.rem(a + (distance + az_size), az_size)

    def ht(distance):
        return lax.rem(r + distance, ht_size)

    barrier = pltpu.get_barrier_semaphore()
    count = 0
    for da in range(-(SPAN - 1), SPAN):
        for dq in range(ht_size):
            if da or dq:
                pl.semaphore_signal(barrier, inc=1, device_id=(az(da), ht(dq)), device_id_type=MESH)
                count += 1

    for wave in range(waves):
        for part in range(2):
            lanes = slice(part * LANES, (part + 1) * LANES)
            first = part * 4 * LANES
            edges[0, wave, :, lanes] = x_ref[wave, :, first : first + LANES]
            edges[1, wave, :, lanes] = x_ref[wave, :, first + 3 * LANES : first + 4 * LANES]
    pl.semaphore_wait(barrier, count)

    def remote(src, dst, send, recv, where):
        return pltpu.make_async_remote_copy(
            src_ref=src, dst_ref=dst, send_sem=send, recv_sem=recv, device_id=where, device_id_type=MESH
        )

    halo_copies = [
        remote(edges.at[side], halo.at[side], sem_hs.at[side], sem_hr.at[side], (az(2 * side - 1), r))
        for side in range(2)
    ]
    for copy in halo_copies:
        copy.start()
    target_copies = [
        remote(target_ref.at[ht(d)], recv_t.at[r], sem_ts.at[d], sem_tr.at[d], (a, ht(d)))
        for d in range(1, ht_size)
    ]
    for copy in target_copies:
        copy.start()
    recv_t[r] = target_ref[r]
    for copy in halo_copies:
        copy.wait_recv()

    def taper(back, block):
        return taper_ref[back * 4 + block : back * 4 + block + 1, :]

    def stage_a(wave, carry):
        lhs = windows(x_ref[wave], halo[1, wave], halo[0, wave])
        y = jnp.dot(lhs, toep_ref[0, wave], preferred_element_type=jnp.float32)
        stack = []
        for back in range(SPAN):
            row = []
            for part in range(2):
                lanes = slice(part * LANES, (part + 1) * LANES)
                for half in range(2):
                    near = y[half * rows : (half + 1) * rows, lanes] * taper(back, half)
                    far = y[(half + 2) * rows : (half + 3) * rows, lanes] * taper(back, half + 2)
                    row.append((near + far).astype(jnp.bfloat16))
            stack.append(jnp.concatenate(row, axis=1))
        folded = jnp.concatenate(stack, axis=0)
        u = jnp.dot(folded, dft_ref[...], preferred_element_type=jnp.float32).astype(jnp.bfloat16)
        for back in range(SPAN):
            for q in range(ht_size):
                send_u[wave, back, q] = u[back * rows : (back + 1) * rows, q * LANES : (q + 1) * LANES]
        for back in range(SPAN - 1, -1, -1):
            for d in range(ht_size):
                if back or d:
                    q = ht(d)
                    remote(
                        send_u.at[wave, back, q], recv_u.at[wave, back, r],
                        sem_us.at[wave, back], sem_ur.at[wave, back], (az(-back), q),
                    ).start()
        recv_u[wave, 0, r] = send_u[wave, 0, r]
        return carry

    def await_bytes(ref, sem):
        pltpu.make_async_copy(ref, ref, sem).wait()

    def group(ref, wave, back):
        first = 1 if back == 0 else 0
        return ref.at[wave, back, pl.ds(0, ht_size - first)]

    lane = lax.broadcasted_iota(jnp.int32, (height, LANES), 1)
    sign = jnp.where(lane < LANES // 2, -1.0, 1.0).astype(jnp.float32)

    def stage_b(wave, carry):
        for back in range(SPAN):
            await_bytes(group(recv_u, wave, back), sem_ur.at[wave, back])
        total = recv_u[wave, 0].astype(jnp.float32)
        for back in range(1, SPAN):
            total = total + recv_u[wave, back].astype(jnp.float32)
        u = total.reshape(height, LANES).astype(jnp.bfloat16)
        z = jnp.dot(prop_ref[wave], u, preferred_element_type=jnp.float32)
        v = z[:height] + sign * pltpu.roll(z[height:], LANES // 2, 1)
        squares = v * v
        power = squares + pltpu.roll(squares, LANES // 2, 1)
        misfit = power - recv_t[:, wave].reshape(height, LANES)
        slope = (2.0 * misfit * v).astype(jnp.bfloat16)
        z = jnp.dot(propt_ref[wave], slope, preferred_element_type=jnp.float32)
        g = z[:height] - sign * pltpu.roll(z[height:], LANES // 2, 1)
        send_g[wave] = g.astype(jnp.bfloat16).reshape(ht_size, rows, LANES)
        for back in range(SPAN - 1, -1, -1):
            for d in range(ht_size):
                if back or d:
                    q = ht(d)
                    remote(
                        send_g.at[wave, q], recv_g.at[wave, back, r],
                        sem_gs.at[wave, back], sem_gr.at[wave, back], (az(back), q),
                    ).start()
        recv_g[wave, 0, r] = send_g[wave, r]
        return carry

    def edge_copy(wave, side):
        return remote(
            gedges.at[wave, side], ghalo.at[wave, side], sem_bs.at[wave, side], sem_br.at[wave, side],
            (az(2 * side - 1), r),
        )

    def stage_c(wave, carry):
        for back in range(SPAN):
            await_bytes(group(recv_g, wave, back), sem_gr.at[wave, back])
        stack = []
        for back in range(SPAN):
            stack.append(jnp.concatenate([recv_g[wave, back, q] for q in range(ht_size)], axis=1))
        lhs = jnp.concatenate(stack, axis=0)
        b = jnp.dot(lhs, idft_ref[...], preferred_element_type=jnp.float32)
        for part in range(2):
            for block in range(4):
                start = (part * 2 + block % 2) * LANES
                total = b[:rows, start : start + LANES] * taper(0, block)
                for back in range(1, SPAN):
                    piece = b[back * rows : (back + 1) * rows, start : start + LANES]
                    total = total + piece * taper(back, block)
                total = total.astype(jnp.bfloat16)
                place = (part * 4 + block) * LANES
                grad[wave, :, place : place + LANES] = total
                if block in (0, 3):
                    lanes = slice(part * LANES, (part + 1) * LANES)
                    gedges[wave, block // 3, :, lanes] = total
        for side in range(2):
            edge_copy(wave, side).start()
        return carry

    def stage_d(wave, carry):
        for side in range(2):
            edge_copy(wave, side).wait()
        lhs = windows(grad[wave], ghalo[wave, 1], ghalo[wave, 0])
        y = jnp.dot(lhs, toep_ref[1, wave], preferred_element_type=jnp.float32)
        for block in range(4):
            for part in range(2):
                place = (part * 4 + block) * LANES
                out_ref[wave, :, place : place + LANES] = y[
                    block * rows : (block + 1) * rows, part * LANES : (part + 1) * LANES
                ]
        for back in range(SPAN):
            first = 1 if back == 0 else 0
            await_bytes(group(send_u, wave, back), sem_us.at[wave, back])
            await_bytes(send_g.at[wave, pl.ds(0, ht_size - first)], sem_gs.at[wave, back])
        return carry

    lax.fori_loop(0, waves, stage_a, 0)
    for copy in target_copies:
        copy.wait()
    lax.fori_loop(0, waves, stage_b, 0)
    lax.fori_loop(0, waves, stage_c, 0)
    lax.fori_loop(0, waves, stage_d, 0)
    for copy in halo_copies:
        copy.wait_send()


def on_device(
    object_field, propagator, kernel_taps, band_reach, sector_offset, sector_width, target_index, target_maps,
    *, az_size, ht_size,
):
    rows, waves, parts, length = object_field.shape
    height = propagator.shape[2]
    here = lax.axis_index("az")
    x = object_field.transpose(1, 0, 2, 3).reshape(waves, rows, parts * length)
    toep = toeplitz_tables(kernel_taps, band_reach)
    tapers = []
    for back in range(SPAN):
        sector = jnp.mod(here - back, az_size)
        tapers.append(taper_row(sector_offset[sector], sector_width[sector], back * length, length))
    tapers = jnp.stack(tapers).reshape(SPAN * length // LANES, LANES)
    dft = dft_table(ht_size)
    prop = propagator.reshape(waves, 2 * height, height)
    propt = propagator.transpose(0, 1, 3, 2).reshape(waves, 2 * height, height)
    plane = lax.dynamic_index_in_dim(target_maps, target_index[here], 0, False)
    plane = plane.reshape(rows, waves, ht_size, FREQS // ht_size).transpose(2, 1, 0, 3)
    plane = jnp.concatenate([plane, plane], axis=3)

    bf16, f32 = jnp.bfloat16, jnp.float32
    dma = pltpu.SemaphoreType.DMA
    vmem = pl.BlockSpec(memory_space=pltpu.VMEM)
    out = pl.pallas_call(
        functools.partial(fused_kernel, az_size, ht_size),
        out_shape=jax.ShapeDtypeStruct((waves, rows, parts * length), f32),
        in_specs=[vmem] * 8,
        out_specs=vmem,
        scratch_shapes=[
            pltpu.VMEM((2, waves, rows, 2 * LANES), bf16),
            pltpu.VMEM((2, waves, rows, 2 * LANES), bf16),
            pltpu.VMEM((waves, SPAN, ht_size, rows, LANES), bf16),
            pltpu.VMEM((waves, SPAN, ht_size, rows, LANES), bf16),
            pltpu.VMEM((ht_size, waves, rows, LANES), f32),
            pltpu.VMEM((waves, ht_size, rows, LANES), bf16),
            pltpu.VMEM((waves, SPAN, ht_size, rows, LANES), bf16),
            pltpu.VMEM((waves, rows, parts * length), bf16),
            pltpu.VMEM((waves, 2, rows, 2 * LANES), bf16),
            pltpu.VMEM((waves, 2, rows, 2 * LANES), bf16),
            dma((2,)), dma((2,)),
            dma((waves, SPAN)), dma((waves, SPAN)),
            dma((ht_size,)), dma((ht_size,)),
            dma((waves, SPAN)), dma((waves, SPAN)),
            dma((waves, 2)), dma((waves, 2)),
        ],
        compiler_params=pltpu.CompilerParams(
            collective_id=0, has_side_effects=True, vmem_limit_bytes=40 * 1024 * 1024
        ),
    )(x, toep, tapers, jnp.asarray(dft), jnp.asarray(np.ascontiguousarray(dft.T)), prop, propt, plane)
    return out.reshape(waves, rows, parts, length).transpose(1, 0, 2, 3)


def solution(mesh):
    in_specs = (P("ht", None, None, "az"), P(), P(), P(), P(), P(), P(), P(None, "ht", None, None))
    out_specs = P("ht", None, None, "az")
    body = functools.partial(on_device, az_size=mesh.shape["az"], ht_size=mesh.shape["ht"])
    return jax.shard_map(body, mesh=mesh, in_specs=in_specs, out_specs=out_specs, check_vma=False)
```

```python
import functools
import math

import jax
import jax.numpy as jnp
import ml_dtypes
import numpy as np
from jax import lax
from jax.experimental import pallas as pl
from jax.experimental.pallas import tpu as pltpu
from jax.sharding import PartitionSpec as P

FREQS = 256
REACH = 64
LANES = 128
SPAN = 4
MESH = pl.DeviceIdType.MESH
ROWS_BY_ROWS = (((1,), (1,)), ((), ()))


def dft_table(quarters):
    index = np.arange(FREQS)
    phases = (index[:, None] * index[None, :] % FREQS) * (2.0 * np.pi / FREQS)
    cosine, sine = np.cos(phases), np.sin(phases)
    table = np.stack([np.stack([cosine, -sine], axis=1), np.stack([sine, cosine], axis=1)], axis=0)
    table = table.reshape(2, FREQS, 2, quarters, FREQS // quarters).transpose(0, 1, 3, 2, 4)
    return table.reshape(2 * FREQS, 2 * FREQS).astype(ml_dtypes.bfloat16)


def forward_toeplitz(row):
    spread = jnp.broadcast_to(row, (LANES, 4 * LANES))
    return pltpu.roll(spread, REACH, 1, stride=1, stride_axis=0)[:, : 3 * LANES]


def backward_toeplitz(row):
    spread = jnp.broadcast_to(row, (3 * LANES, 4 * LANES))
    return pltpu.roll(spread, 5 * REACH, 1, stride=1, stride_axis=0)[:, :LANES]


def windows(own, left, right):
    stack = []
    for block in range(4):
        row = []
        for part in range(2):
            for near in (block - 1, block, block + 1):
                if near < 0:
                    row.append(left[:, part * LANES : (part + 1) * LANES])
                elif near > 3:
                    row.append(right[:, part * LANES : (part + 1) * LANES])
                else:
                    start = (part * 4 + near) * LANES
                    row.append(own[:, start : start + LANES])
        stack.append(jnp.concatenate(row, axis=1))
    return jnp.concatenate(stack, axis=0)


def fused_kernel(
    az_size, ht_size, x_ref, taps_ref, reach_ref, offset_ref, width_ref, dft_hbm, prop_hbm, propt_hbm,
    target_ref, out_ref, dft_ref, prop_ref, propt_ref, taper_ref, padded, front, behind, edges, halo, send_u, recv_u, recv_t, send_g, recv_g, grad, gedges, ghalo,
    sem_hs, sem_hr, sem_us, sem_ur, sem_ts, sem_tr, sem_gs, sem_gr, sem_bs, sem_br, sem_in,
):
    a = lax.axis_index("az")
    r = lax.axis_index("ht")
    waves, rows, _ = x_ref.shape
    height = rows * ht_size

    def az(distance):
        return lax.rem(a + (distance + az_size), az_size)

    def ht(distance):
        return lax.rem(r + distance, ht_size)

    loads = [
        pltpu.make_async_copy(src, dst, sem_in.at[i])
        for i, (src, dst) in enumerate(((dft_hbm, dft_ref), (prop_hbm, prop_ref), (propt_hbm, propt_ref)))
    ]
    for load in loads:
        load.start()

    barrier = pltpu.get_barrier_semaphore()
    count = 0
    for da in range(-(SPAN - 1), SPAN):
        for dq in range(ht_size):
            if da or dq:
                pl.semaphore_signal(barrier, inc=1, device_id=(az(da), ht(dq)), device_id_type=MESH)
                count += 1

    for wave in range(waves):
        for part in range(2):
            lanes = slice(part * LANES, (part + 1) * LANES)
            first = part * 4 * LANES
            edges[0, wave, :, lanes] = x_ref[wave, :, first : first + LANES]
            edges[1, wave, :, lanes] = x_ref[wave, :, first + 3 * LANES : first + 4 * LANES]
    pl.semaphore_wait(barrier, count)

    def remote(src, dst, send, recv, where):
        return pltpu.make_async_remote_copy(
            src_ref=src, dst_ref=dst, send_sem=send, recv_sem=recv, device_id=where, device_id_type=MESH
        )

    halo_copies = [
        remote(edges.at[side], halo.at[side], sem_hs.at[side], sem_hr.at[side], (az(2 * side - 1), r))
        for side in range(2)
    ]
    for copy in halo_copies:
        copy.start()
    target_copies = [
        remote(target_ref.at[ht(d)], recv_t.at[r], sem_ts.at[d], sem_tr.at[d], (a, ht(d)))
        for d in range(1, ht_size)
    ]
    for copy in target_copies:
        copy.start()
    recv_t[r] = target_ref[r]

    blocks = lax.broadcasted_iota(jnp.int32, (4, LANES), 0) * LANES
    spots = blocks + lax.broadcasted_iota(jnp.int32, (4, LANES), 1)
    for back in range(SPAN):
        width = width_ref[az(-back)]
        places = spots + (4 * back * LANES - offset_ref[az(-back)])
        inside = (places >= 0) & (places < width)
        places = jnp.where(inside, places, 0).astype(jnp.float32)
        span = jnp.full((4, LANES), width, jnp.int32).astype(jnp.float32)
        taper = 0.5 - 0.5 * jnp.cos((places + 0.5) * (2.0 * math.pi) / span)
        taper_ref[4 * back : 4 * back + 4, :] = jnp.where(inside, taper, 0.0) / jnp.sqrt(span)

    taps_count = 2 * REACH + 1
    distance = jnp.abs(lax.broadcasted_iota(jnp.int32, (2, 4 * LANES), 1) - REACH)
    padded[...] = jnp.zeros_like(padded)
    for wave in range(waves):
        padded[wave, :, :taps_count] = taps_ref[wave]
        rows_of = jnp.where(distance <= reach_ref[wave], padded[wave], 0.0)
        padded[wave] = rows_of
        real = forward_toeplitz(rows_of[0:1])
        imag = forward_toeplitz(rows_of[1:2])
        front[wave, :LANES] = jnp.concatenate([real, -imag], axis=1).astype(jnp.bfloat16)
        front[wave, LANES:] = jnp.concatenate([imag, real], axis=1).astype(jnp.bfloat16)

    loads[0].wait()
    for copy in halo_copies:
        copy.wait_recv()

    def taper(back, block):
        return taper_ref[back * 4 + block : back * 4 + block + 1, :]

    def stage_a(wave, carry):
        lhs = windows(x_ref[wave], halo[1, wave], halo[0, wave])
        y = lax.dot_general(lhs, front[wave], ROWS_BY_ROWS, preferred_element_type=jnp.float32)
        stack = []
        for back in range(SPAN):
            row = []
            for part in range(2):
                lanes = slice(part * LANES, (part + 1) * LANES)
                for half in range(2):
                    near = y[half * rows : (half + 1) * rows, lanes] * taper(back, half)
                    far = y[(half + 2) * rows : (half + 3) * rows, lanes] * taper(back, half + 2)
                    row.append((near + far).astype(jnp.bfloat16))
            stack.append(jnp.concatenate(row, axis=1))
        folded = jnp.concatenate(stack, axis=0)
        u = jnp.dot(folded, dft_ref[...], preferred_element_type=jnp.float32).astype(jnp.bfloat16)
        for back in range(SPAN):
            for q in range(ht_size):
                send_u[wave, back, q] = u[back * rows : (back + 1) * rows, q * LANES : (q + 1) * LANES]
        for back in range(SPAN - 1, -1, -1):
            for d in range(ht_size):
                if back or d:
                    q = ht(d)
                    remote(
                        send_u.at[wave, back, q], recv_u.at[wave, back, r],
                        sem_us.at[wave, back], sem_ur.at[wave, back], (az(-back), q),
                    ).start()
        recv_u[wave, 0, r] = send_u[wave, 0, r]
        return carry

    def await_bytes(ref, sem):
        pltpu.make_async_copy(ref, ref, sem).wait()

    def group(ref, wave, back):
        first = 1 if back == 0 else 0
        return ref.at[wave, back, pl.ds(0, ht_size - first)]

    lane = lax.broadcasted_iota(jnp.int32, (height, LANES), 1)
    sign = jnp.where(lane < LANES // 2, -1.0, 1.0).astype(jnp.float32)

    def stage_b(wave, carry):
        for back in range(SPAN):
            await_bytes(group(recv_u, wave, back), sem_ur.at[wave, back])
        total = recv_u[wave, 0].astype(jnp.float32)
        for back in range(1, SPAN):
            total = total + recv_u[wave, back].astype(jnp.float32)
        u = total.reshape(height, LANES).astype(jnp.bfloat16)
        z = jnp.dot(prop_ref[wave], u, preferred_element_type=jnp.float32)
        v = z[:height] + sign * pltpu.roll(z[height:], LANES // 2, 1)
        squares = v * v
        power = squares + pltpu.roll(squares, LANES // 2, 1)
        misfit = power - recv_t[:, wave].reshape(height, LANES)
        slope = (2.0 * misfit * v).astype(jnp.bfloat16)
        z = jnp.dot(propt_ref[wave], slope, preferred_element_type=jnp.float32)
        g = z[:height] - sign * pltpu.roll(z[height:], LANES // 2, 1)
        send_g[wave] = g.astype(jnp.bfloat16).reshape(ht_size, rows, LANES)
        for back in range(SPAN - 1, -1, -1):
            for d in range(ht_size):
                if back or d:
                    q = ht(d)
                    remote(
                        send_g.at[wave, q], recv_g.at[wave, back, r],
                        sem_gs.at[wave, back], sem_gr.at[wave, back], (az(back), q),
                    ).start()
        recv_g[wave, 0, r] = send_g[wave, r]
        return carry

    def edge_copy(wave, side):
        return remote(
            gedges.at[wave, side], ghalo.at[wave, side], sem_bs.at[wave, side], sem_br.at[wave, side],
            (az(2 * side - 1), r),
        )

    def stage_c(wave, carry):
        for back in range(SPAN):
            await_bytes(group(recv_g, wave, back), sem_gr.at[wave, back])
        stack = []
        for back in range(SPAN):
            stack.append(jnp.concatenate([recv_g[wave, back, q] for q in range(ht_size)], axis=1))
        lhs = jnp.concatenate(stack, axis=0)
        b = lax.dot_general(lhs, dft_ref[...], ROWS_BY_ROWS, preferred_element_type=jnp.float32)
        for part in range(2):
            for block in range(4):
                start = (part * 2 + block % 2) * LANES
                total = b[:rows, start : start + LANES] * taper(0, block)
                for back in range(1, SPAN):
                    piece = b[back * rows : (back + 1) * rows, start : start + LANES]
                    total = total + piece * taper(back, block)
                total = total.astype(jnp.bfloat16)
                place = (part * 4 + block) * LANES
                grad[wave, :, place : place + LANES] = total
                if block in (0, 3):
                    lanes = slice(part * LANES, (part + 1) * LANES)
                    gedges[wave, block // 3, :, lanes] = total
        for side in range(2):
            edge_copy(wave, side).start()
        return carry

    def stage_d(wave, carry):
        for side in range(2):
            edge_copy(wave, side).wait()
        lhs = windows(grad[wave], ghalo[wave, 1], ghalo[wave, 0])
        y = jnp.dot(lhs, behind[wave], preferred_element_type=jnp.float32)
        for block in range(4):
            for part in range(2):
                place = (part * 4 + block) * LANES
                out_ref[wave, :, place : place + LANES] = y[
                    block * rows : (block + 1) * rows, part * LANES : (part + 1) * LANES
                ]
        for back in range(SPAN):
            first = 1 if back == 0 else 0
            await_bytes(group(send_u, wave, back), sem_us.at[wave, back])
            await_bytes(send_g.at[wave, pl.ds(0, ht_size - first)], sem_gs.at[wave, back])
        return carry

    lax.fori_loop(0, waves, stage_a, 0)
    for wave in range(waves):
        real = backward_toeplitz(padded[wave, 0:1, :])
        imag = backward_toeplitz(padded[wave, 1:2, :])
        behind[wave, : 3 * LANES] = jnp.concatenate([real, -imag], axis=1).astype(jnp.bfloat16)
        behind[wave, 3 * LANES :] = jnp.concatenate([imag, real], axis=1).astype(jnp.bfloat16)
    for load in loads[1:]:
        load.wait()
    for copy in target_copies:
        copy.wait()
    lax.fori_loop(0, waves, stage_b, 0)
    lax.fori_loop(0, waves, stage_c, 0)
    lax.fori_loop(0, waves, stage_d, 0)
    for copy in halo_copies:
        copy.wait_send()


def on_device(
    object_field, propagator, kernel_taps, band_reach, sector_offset, sector_width, target_index, target_maps,
    *, az_size, ht_size,
):
    rows, waves, parts, length = object_field.shape
    height = propagator.shape[2]
    here = lax.axis_index("az")
    x = object_field.transpose(1, 0, 2, 3).reshape(waves, rows, parts * length)
    dft = jnp.asarray(dft_table(ht_size))
    prop = propagator.reshape(waves, 2 * height, height)
    propt = propagator.transpose(0, 1, 3, 2).reshape(waves, 2 * height, height)
    plane = lax.dynamic_index_in_dim(target_maps, target_index[here], 0, False)
    plane = plane.reshape(rows, waves, ht_size, FREQS // ht_size).transpose(2, 1, 0, 3)
    plane = jnp.concatenate([plane, plane], axis=3)

    bf16, f32 = jnp.bfloat16, jnp.float32
    dma = pltpu.SemaphoreType.DMA
    vmem = pl.BlockSpec(memory_space=pltpu.VMEM)
    smem = pl.BlockSpec(memory_space=pltpu.SMEM)
    hbm = pl.BlockSpec(memory_space=pltpu.HBM)
    out = pl.pallas_call(
        functools.partial(fused_kernel, az_size, ht_size),
        out_shape=jax.ShapeDtypeStruct((waves, rows, parts * length), f32),
        in_specs=[vmem, vmem, smem, smem, smem, hbm, hbm, hbm, vmem],
        out_specs=vmem,
        scratch_shapes=[
            pltpu.VMEM(dft.shape, bf16),
            pltpu.VMEM(prop.shape, bf16),
            pltpu.VMEM(propt.shape, bf16),
            pltpu.VMEM((4 * SPAN, LANES), f32),
            pltpu.VMEM((waves, 2, 4 * LANES), f32),
            pltpu.VMEM((waves, 2 * LANES, 6 * LANES), bf16),
            pltpu.VMEM((waves, 6 * LANES, 2 * LANES), bf16),
            pltpu.VMEM((2, waves, rows, 2 * LANES), bf16),
            pltpu.VMEM((2, waves, rows, 2 * LANES), bf16),
            pltpu.VMEM((waves, SPAN, ht_size, rows, LANES), bf16),
            pltpu.VMEM((waves, SPAN, ht_size, rows, LANES), bf16),
            pltpu.VMEM((ht_size, waves, rows, LANES), f32),
            pltpu.VMEM((waves, ht_size, rows, LANES), bf16),
            pltpu.VMEM((waves, SPAN, ht_size, rows, LANES), bf16),
            pltpu.VMEM((waves, rows, parts * length), bf16),
            pltpu.VMEM((waves, 2, rows, 2 * LANES), bf16),
            pltpu.VMEM((waves, 2, rows, 2 * LANES), bf16),
            dma((2,)), dma((2,)),
            dma((waves, SPAN)), dma((waves, SPAN)),
            dma((ht_size,)), dma((ht_size,)),
            dma((waves, SPAN)), dma((waves, SPAN)),
            dma((waves, 2)), dma((waves, 2)), dma((3,)),
        ],
        compiler_params=pltpu.CompilerParams(
            collective_id=0, has_side_effects=True, vmem_limit_bytes=40 * 1024 * 1024
        ),
    )(x, kernel_taps, band_reach, sector_offset, sector_width, dft, prop, propt, plane)
    return out.reshape(waves, rows, parts, length).transpose(1, 0, 2, 3)


def solution(mesh):
    in_specs = (P("ht", None, None, "az"), P(), P(), P(), P(), P(), P(), P(None, "ht", None, None))
    out_specs = P("ht", None, None, "az")
    body = functools.partial(on_device, az_size=mesh.shape["az"], ht_size=mesh.shape["ht"])
    return jax.shard_map(body, mesh=mesh, in_specs=in_specs, out_specs=out_specs, check_vma=False)
```

```python
import functools
import math

import jax
import jax.numpy as jnp
import ml_dtypes
import numpy as np
from jax import lax
from jax.experimental import pallas as pl
from jax.experimental.pallas import tpu as pltpu
from jax.sharding import PartitionSpec as P

FREQS = 256
REACH = 64
LANES = 128
SPAN = 4
MESH = pl.DeviceIdType.MESH
ROWS_BY_ROWS = (((1,), (1,)), ((), ()))


def dft_table(quarters):
    index = np.arange(FREQS)
    phases = (index[:, None] * index[None, :] % FREQS) * (2.0 * np.pi / FREQS)
    cosine, sine = np.cos(phases), np.sin(phases)
    table = np.stack([np.stack([cosine, -sine], axis=1), np.stack([sine, cosine], axis=1)], axis=0)
    table = table.reshape(2, FREQS, 2, quarters, FREQS // quarters).transpose(0, 1, 3, 2, 4)
    return table.reshape(2 * FREQS, 2 * FREQS).astype(ml_dtypes.bfloat16)


def forward_toeplitz(row):
    spread = jnp.broadcast_to(row, (LANES, 4 * LANES))
    return pltpu.roll(spread, REACH, 1, stride=1, stride_axis=0)[:, : 3 * LANES]


def backward_toeplitz(row):
    spread = jnp.broadcast_to(row, (3 * LANES, 4 * LANES))
    return pltpu.roll(spread, 5 * REACH, 1, stride=1, stride_axis=0)[:, :LANES]


def windows(own, left, right):
    stack = []
    for block in range(4):
        row = []
        for part in range(2):
            for near in (block - 1, block, block + 1):
                if near < 0:
                    row.append(left[:, part * LANES : (part + 1) * LANES])
                elif near > 3:
                    row.append(right[:, part * LANES : (part + 1) * LANES])
                else:
                    start = (part * 4 + near) * LANES
                    row.append(own[:, start : start + LANES])
        stack.append(jnp.concatenate(row, axis=1))
    return jnp.concatenate(stack, axis=0)


def fused_kernel(
    az_size, ht_size, x_hbm, taps_ref, reach_ref, offset_ref, width_ref, dft_hbm, prop_hbm, propt_hbm,
    target_ref, out_ref, x_ref, dft_ref, prop_ref, propt_ref, taper_ref, padded, front, behind, relay, edges, halo, send_u, recv_u, recv_t, send_g, recv_g, grad, gedges, ghalo,
    sem_hs, sem_hr, sem_us, sem_ur, sem_ts, sem_tr, sem_gs, sem_gr, sem_bs, sem_br, sem_rs, sem_rr, sem_in,
):
    a = lax.axis_index("az")
    r = lax.axis_index("ht")
    waves, rows, _ = x_ref.shape
    height = rows * ht_size

    def az(distance):
        return lax.rem(a + (distance + az_size), az_size)

    def ht(distance):
        return lax.rem(r + distance, ht_size)

    pairs = (
        (x_hbm, x_ref), (dft_hbm, dft_ref), (prop_hbm, prop_ref), (propt_hbm, propt_ref),
        (target_ref.at[r], recv_t.at[r]),
    )
    loads = [
        pltpu.make_async_copy(src, dst, sem_in.at[i])
        for i, (src, dst) in enumerate(pairs)
    ]
    for load in loads:
        load.start()

    barrier = pltpu.get_barrier_semaphore()
    count = 0
    for da in range(-2, 3):
        for dq in range(ht_size):
            if da or dq:
                pl.semaphore_signal(barrier, inc=1, device_id=(az(da), ht(dq)), device_id_type=MESH)
                count += 1

    loads[0].wait()
    for wave in range(waves):
        for part in range(2):
            lanes = slice(part * LANES, (part + 1) * LANES)
            first = part * 4 * LANES
            edges[0, wave, :, lanes] = x_ref[wave, :, first : first + LANES]
            edges[1, wave, :, lanes] = x_ref[wave, :, first + 3 * LANES : first + 4 * LANES]
    pl.semaphore_wait(barrier, count)

    def remote(src, dst, send, recv, where):
        return pltpu.make_async_remote_copy(
            src_ref=src, dst_ref=dst, send_sem=send, recv_sem=recv, device_id=where, device_id_type=MESH
        )

    halo_copies = [
        remote(edges.at[side], halo.at[side], sem_hs.at[side], sem_hr.at[side], (az(2 * side - 1), r))
        for side in range(2)
    ]
    for copy in halo_copies:
        copy.start()
    target_copies = [
        remote(target_ref.at[ht(d)], recv_t.at[r], sem_ts.at[d], sem_tr.at[d], (a, ht(d)))
        for d in range(1, ht_size)
    ]
    for copy in target_copies:
        copy.start()

    blocks = lax.broadcasted_iota(jnp.int32, (4, LANES), 0) * LANES
    spots = blocks + lax.broadcasted_iota(jnp.int32, (4, LANES), 1)
    for back in range(SPAN):
        width = width_ref[az(-back)]
        places = spots + (4 * back * LANES - offset_ref[az(-back)])
        inside = (places >= 0) & (places < width)
        places = jnp.where(inside, places, 0).astype(jnp.float32)
        span = jnp.full((4, LANES), width, jnp.int32).astype(jnp.float32)
        taper = 0.5 - 0.5 * jnp.cos((places + 0.5) * (2.0 * math.pi) / span)
        taper_ref[4 * back : 4 * back + 4, :] = jnp.where(inside, taper, 0.0) / jnp.sqrt(span)

    taps_count = 2 * REACH + 1
    distance = jnp.abs(lax.broadcasted_iota(jnp.int32, (2, 4 * LANES), 1) - REACH)
    padded[...] = jnp.zeros_like(padded)
    for wave in range(waves):
        padded[wave, :, :taps_count] = taps_ref[wave]
        rows_of = jnp.where(distance <= reach_ref[wave], padded[wave], 0.0)
        padded[wave] = rows_of
        real = forward_toeplitz(rows_of[0:1])
        imag = forward_toeplitz(rows_of[1:2])
        front[wave, :LANES] = jnp.concatenate([real, -imag], axis=1).astype(jnp.bfloat16)
        front[wave, LANES:] = jnp.concatenate([imag, real], axis=1).astype(jnp.bfloat16)

    loads[1].wait()
    for copy in halo_copies:
        copy.wait_recv()

    def taper(back, block):
        return taper_ref[back * 4 + block : back * 4 + block + 1, :]

    def relay_copy(wave):
        return remote(send_u.at[wave, 3], relay.at[wave], sem_us.at[wave, 3], sem_ur.at[wave, 3], (az(-1), r))

    def spread_u(wave, back):
        for d in range(ht_size):
            if back or d:
                q = ht(d)
                remote(
                    send_u.at[wave, back, q], recv_u.at[wave, back, r],
                    sem_us.at[wave, back], sem_ur.at[wave, back], (az(-back), q),
                ).start()

    def stage_a(wave, carry):
        lhs = windows(x_ref[wave], halo[1, wave], halo[0, wave])
        y = lax.dot_general(lhs, front[wave], ROWS_BY_ROWS, preferred_element_type=jnp.float32)
        stack = []
        for back in range(SPAN):
            row = []
            for part in range(2):
                lanes = slice(part * LANES, (part + 1) * LANES)
                for half in range(2):
                    near = y[half * rows : (half + 1) * rows, lanes] * taper(back, half)
                    far = y[(half + 2) * rows : (half + 3) * rows, lanes] * taper(back, half + 2)
                    row.append((near + far).astype(jnp.bfloat16))
            stack.append(jnp.concatenate(row, axis=1))
        folded = jnp.concatenate(stack, axis=0)
        u = jnp.dot(folded, dft_ref[...], preferred_element_type=jnp.float32).astype(jnp.bfloat16)
        for back in range(SPAN):
            for q in range(ht_size):
                send_u[wave, back, q] = u[back * rows : (back + 1) * rows, q * LANES : (q + 1) * LANES]
        relay_copy(wave).start()
        spread_u(wave, 1)
        spread_u(wave, 0)
        recv_u[wave, 0, r] = send_u[wave, 0, r]
        return carry

    def stage_r(wave, carry):
        relay_copy(wave).wait_recv()
        both = send_u[wave, 2].astype(jnp.float32) + relay[wave].astype(jnp.float32)
        send_u[wave, 2] = both.astype(jnp.bfloat16)
        spread_u(wave, 2)
        return carry

    def await_bytes(ref, sem):
        pltpu.make_async_copy(ref, ref, sem).wait()

    def group(ref, wave, back):
        first = 1 if back == 0 else 0
        return ref.at[wave, back, pl.ds(0, ht_size - first)]

    lane = lax.broadcasted_iota(jnp.int32, (height, LANES), 1)
    sign = jnp.where(lane < LANES // 2, -1.0, 1.0).astype(jnp.float32)

    def stage_b(wave, carry):
        for back in range(3):
            await_bytes(group(recv_u, wave, back), sem_ur.at[wave, back])
        total = recv_u[wave, 0].astype(jnp.float32)
        for back in range(1, 3):
            total = total + recv_u[wave, back].astype(jnp.float32)
        u = total.reshape(height, LANES).astype(jnp.bfloat16)
        z = jnp.dot(prop_ref[wave], u, preferred_element_type=jnp.float32)
        v = z[:height] + sign * pltpu.roll(z[height:], LANES // 2, 1)
        squares = v * v
        power = squares + pltpu.roll(squares, LANES // 2, 1)
        misfit = power - recv_t[:, wave].reshape(height, LANES)
        slope = (2.0 * misfit * v).astype(jnp.bfloat16)
        z = jnp.dot(propt_ref[wave], slope, preferred_element_type=jnp.float32)
        g = z[:height] - sign * pltpu.roll(z[height:], LANES // 2, 1)
        send_g[wave] = g.astype(jnp.bfloat16).reshape(ht_size, rows, LANES)
        for back in (2, 1, 0):
            for d in range(ht_size):
                if back or d:
                    q = ht(d)
                    remote(
                        send_g.at[wave, q], recv_g.at[wave, back, r],
                        sem_gs.at[wave, back], sem_gr.at[wave, back], (az(back), q),
                    ).start()
        recv_g[wave, 0, r] = send_g[wave, r]
        return carry

    def pass_copy(wave):
        return remote(
            recv_g.at[wave, 2], recv_g.at[wave, 3], sem_rs.at[wave], sem_rr.at[wave], (az(1), r)
        )

    def stage_x(wave, carry):
        await_bytes(group(recv_g, wave, 2), sem_gr.at[wave, 2])
        pass_copy(wave).start()
        return carry

    def edge_copy(wave, side):
        return remote(
            gedges.at[wave, side], ghalo.at[wave, side], sem_bs.at[wave, side], sem_br.at[wave, side],
            (az(2 * side - 1), r),
        )

    def stage_c(wave, carry):
        for back in range(2):
            await_bytes(group(recv_g, wave, back), sem_gr.at[wave, back])
        pass_copy(wave).wait_recv()
        stack = []
        for back in range(SPAN):
            stack.append(jnp.concatenate([recv_g[wave, back, q] for q in range(ht_size)], axis=1))
        lhs = jnp.concatenate(stack, axis=0)
        b = lax.dot_general(lhs, dft_ref[...], ROWS_BY_ROWS, preferred_element_type=jnp.float32)
        for part in range(2):
            for block in range(4):
                start = (part * 2 + block % 2) * LANES
                total = b[:rows, start : start + LANES] * taper(0, block)
                for back in range(1, SPAN):
                    piece = b[back * rows : (back + 1) * rows, start : start + LANES]
                    total = total + piece * taper(back, block)
                total = total.astype(jnp.bfloat16)
                place = (part * 4 + block) * LANES
                grad[wave, :, place : place + LANES] = total
                if block in (0, 3):
                    lanes = slice(part * LANES, (part + 1) * LANES)
                    gedges[wave, block // 3, :, lanes] = total
        for side in range(2):
            edge_copy(wave, side).start()
        return carry

    def stage_d(wave, carry):
        for side in range(2):
            edge_copy(wave, side).wait()
        lhs = windows(grad[wave], ghalo[wave, 1], ghalo[wave, 0])
        y = jnp.dot(lhs, behind[wave], preferred_element_type=jnp.float32)
        for block in range(4):
            for part in range(2):
                place = (part * 4 + block) * LANES
                out_ref[wave, :, place : place + LANES] = y[
                    block * rows : (block + 1) * rows, part * LANES : (part + 1) * LANES
                ]
        for back in range(SPAN):
            first = 1 if back == 0 else 0
            await_bytes(group(send_u, wave, back), sem_us.at[wave, back])
            if back < 3:
                await_bytes(send_g.at[wave, pl.ds(0, ht_size - first)], sem_gs.at[wave, back])
        pass_copy(wave).wait_send()
        return carry

    def ahead(wave, carry):
        stage_a(wave, 0)
        lax.cond(wave > 0, lambda: stage_r(wave - 1, 0), lambda: 0)
        return carry

    def middle(step, carry):
        lax.cond(step < waves, lambda: stage_b(step, 0), lambda: 0)
        lax.cond((step > 0) & (step <= waves), lambda: stage_x(step - 1, 0), lambda: 0)
        lax.cond((step > 1) & (step <= waves + 1), lambda: stage_c(step - 2, 0), lambda: 0)
        lax.cond(step > 2, lambda: stage_d(step - 3, 0), lambda: 0)
        return carry

    lax.fori_loop(0, waves, ahead, 0)
    stage_r(waves - 1, 0)
    for wave in range(waves):
        real = backward_toeplitz(padded[wave, 0:1, :])
        imag = backward_toeplitz(padded[wave, 1:2, :])
        behind[wave, : 3 * LANES] = jnp.concatenate([real, -imag], axis=1).astype(jnp.bfloat16)
        behind[wave, 3 * LANES :] = jnp.concatenate([imag, real], axis=1).astype(jnp.bfloat16)
    for load in loads[2:]:
        load.wait()
    for copy in target_copies:
        copy.wait()
    lax.fori_loop(0, waves + 3, middle, 0)
    for copy in halo_copies:
        copy.wait_send()


def on_device(
    object_field, propagator, kernel_taps, band_reach, sector_offset, sector_width, target_index, target_maps,
    *, az_size, ht_size,
):
    rows, waves, parts, length = object_field.shape
    height = propagator.shape[2]
    here = lax.axis_index("az")
    x = object_field.transpose(1, 0, 2, 3).reshape(waves, rows, parts * length)
    dft = jnp.asarray(dft_table(ht_size))
    prop = propagator.reshape(waves, 2 * height, height)
    propt = propagator.transpose(0, 1, 3, 2).reshape(waves, 2 * height, height)
    plane = lax.dynamic_index_in_dim(target_maps, target_index[here], 0, False)
    plane = plane.reshape(rows, waves, ht_size, FREQS // ht_size).transpose(2, 1, 0, 3)
    plane = jnp.concatenate([plane, plane], axis=3)

    bf16, f32 = jnp.bfloat16, jnp.float32
    dma = pltpu.SemaphoreType.DMA
    vmem = pl.BlockSpec(memory_space=pltpu.VMEM)
    smem = pl.BlockSpec(memory_space=pltpu.SMEM)
    hbm = pl.BlockSpec(memory_space=pltpu.HBM)
    out = pl.pallas_call(
        functools.partial(fused_kernel, az_size, ht_size),
        out_shape=jax.ShapeDtypeStruct((waves, rows, parts * length), f32),
        in_specs=[hbm, vmem, smem, smem, smem, hbm, hbm, hbm, hbm],
        out_specs=vmem,
        scratch_shapes=[
            pltpu.VMEM(x.shape, bf16),
            pltpu.VMEM(dft.shape, bf16),
            pltpu.VMEM(prop.shape, bf16),
            pltpu.VMEM(propt.shape, bf16),
            pltpu.VMEM((4 * SPAN, LANES), f32),
            pltpu.VMEM((waves, 2, 4 * LANES), f32),
            pltpu.VMEM((waves, 2 * LANES, 6 * LANES), bf16),
            pltpu.VMEM((waves, 6 * LANES, 2 * LANES), bf16),
            pltpu.VMEM((waves, ht_size, rows, LANES), bf16),
            pltpu.VMEM((2, waves, rows, 2 * LANES), bf16),
            pltpu.VMEM((2, waves, rows, 2 * LANES), bf16),
            pltpu.VMEM((waves, SPAN, ht_size, rows, LANES), bf16),
            pltpu.VMEM((waves, SPAN, ht_size, rows, LANES), bf16),
            pltpu.VMEM((ht_size, waves, rows, LANES), f32),
            pltpu.VMEM((waves, ht_size, rows, LANES), bf16),
            pltpu.VMEM((waves, SPAN, ht_size, rows, LANES), bf16),
            pltpu.VMEM((waves, rows, parts * length), bf16),
            pltpu.VMEM((waves, 2, rows, 2 * LANES), bf16),
            pltpu.VMEM((waves, 2, rows, 2 * LANES), bf16),
            dma((2,)), dma((2,)),
            dma((waves, SPAN)), dma((waves, SPAN)),
            dma((ht_size,)), dma((ht_size,)),
            dma((waves, SPAN)), dma((waves, SPAN)),
            dma((waves, 2)), dma((waves, 2)), dma((waves,)), dma((waves,)), dma((5,)),
        ],
        compiler_params=pltpu.CompilerParams(
            collective_id=0, has_side_effects=True, vmem_limit_bytes=60 * 1024 * 1024
        ),
    )(x, kernel_taps, band_reach, sector_offset, sector_width, dft, prop, propt, plane)
    return out.reshape(waves, rows, parts, length).transpose(1, 0, 2, 3)


def solution(mesh):
    in_specs = (P("ht", None, None, "az"), P(), P(), P(), P(), P(), P(), P(None, "ht", None, None))
    out_specs = P("ht", None, None, "az")
    body = functools.partial(on_device, az_size=mesh.shape["az"], ht_size=mesh.shape["ht"])
    return jax.shard_map(body, mesh=mesh, in_specs=in_specs, out_specs=out_specs, check_vma=False)
```

```python
import functools
import math

import jax
import jax.numpy as jnp
import ml_dtypes
import numpy as np
from jax import lax
from jax.experimental import pallas as pl
from jax.experimental.pallas import tpu as pltpu
from jax.sharding import PartitionSpec as P

FREQS = 256
REACH = 64
LANES = 128
SPAN = 4
MESH = pl.DeviceIdType.MESH
ROWS_BY_ROWS = (((1,), (1,)), ((), ()))


def dft_table(quarters):
    index = np.arange(FREQS)
    phases = (index[:, None] * index[None, :] % FREQS) * (2.0 * np.pi / FREQS)
    cosine, sine = np.cos(phases), np.sin(phases)
    table = np.stack([np.stack([cosine, -sine], axis=1), np.stack([sine, cosine], axis=1)], axis=0)
    table = table.reshape(2, FREQS, 2, quarters, FREQS // quarters).transpose(0, 1, 3, 2, 4)
    return table.reshape(2 * FREQS, 2 * FREQS).astype(ml_dtypes.bfloat16)


def forward_toeplitz(row):
    spread = jnp.broadcast_to(row, (LANES, 4 * LANES))
    return pltpu.roll(spread, REACH, 1, stride=1, stride_axis=0)[:, : 3 * LANES]


def backward_toeplitz(row):
    spread = jnp.broadcast_to(row, (3 * LANES, 4 * LANES))
    return pltpu.roll(spread, 5 * REACH, 1, stride=1, stride_axis=0)[:, :LANES]


def windows(own, left, right):
    stack = []
    for block in range(4):
        row = []
        for part in range(2):
            for near in (block - 1, block, block + 1):
                if near < 0:
                    row.append(left[:, part * LANES : (part + 1) * LANES])
                elif near > 3:
                    row.append(right[:, part * LANES : (part + 1) * LANES])
                else:
                    start = (part * 4 + near) * LANES
                    row.append(own[:, start : start + LANES])
        stack.append(jnp.concatenate(row, axis=1))
    return jnp.concatenate(stack, axis=0)


def fused_kernel(
    az_size, ht_size, x_hbm, taps_ref, reach_ref, offset_ref, width_ref, dft_hbm, prop_hbm, propt_hbm,
    index_ref, maps_ref, out_ref, target_ref, x_ref, dft_ref, prop_ref, propt_ref, taper_ref, padded, front, behind, relay, edges, halo, send_u, recv_u, recv_t, send_g, recv_g, grad, gedges, ghalo,
    sem_hs, sem_hr, sem_us, sem_ur, sem_ts, sem_tr, sem_gs, sem_gr, sem_bs, sem_br, sem_rs, sem_rr, sem_in,
):
    a = lax.axis_index("az")
    r = lax.axis_index("ht")
    waves, rows, _ = x_ref.shape
    height = rows * ht_size

    def az(distance):
        return lax.rem(a + (distance + az_size), az_size)

    def ht(distance):
        return lax.rem(r + distance, ht_size)

    pairs = (
        (x_hbm, x_ref), (dft_hbm, dft_ref), (prop_hbm, prop_ref), (propt_hbm, propt_ref),
    )
    loads = [
        pltpu.make_async_copy(src, dst, sem_in.at[i])
        for i, (src, dst) in enumerate(pairs)
    ]
    for load in loads:
        load.start()

    barrier = pltpu.get_barrier_semaphore()
    count = 0
    for da in range(-2, 3):
        for dq in range(ht_size):
            if da or dq:
                pl.semaphore_signal(barrier, inc=1, device_id=(az(da), ht(dq)), device_id_type=MESH)
                count += 1

    loads[0].wait()
    for wave in range(waves):
        for part in range(2):
            lanes = slice(part * LANES, (part + 1) * LANES)
            first = part * 4 * LANES
            edges[0, wave, :, lanes] = x_ref[wave, :, first : first + LANES]
            edges[1, wave, :, lanes] = x_ref[wave, :, first + 3 * LANES : first + 4 * LANES]
    pl.semaphore_wait(barrier, count)

    def remote(src, dst, send, recv, where):
        return pltpu.make_async_remote_copy(
            src_ref=src, dst_ref=dst, send_sem=send, recv_sem=recv, device_id=where, device_id_type=MESH
        )

    halo_copies = [
        remote(edges.at[side], halo.at[side], sem_hs.at[side], sem_hr.at[side], (az(2 * side - 1), r))
        for side in range(2)
    ]
    for copy in halo_copies:
        copy.start()
    pattern = index_ref[a]
    half = LANES // 2
    for wave in range(waves):
        plane = maps_ref[pattern, wave]
        for q in range(ht_size):
            piece = plane[:, q * half : (q + 1) * half]
            target_ref[q, wave] = jnp.concatenate([piece, piece], axis=1)
    recv_t[r] = target_ref[r]
    target_copies = [
        remote(target_ref.at[ht(d)], recv_t.at[r], sem_ts.at[d], sem_tr.at[d], (a, ht(d)))
        for d in range(1, ht_size)
    ]
    for copy in target_copies:
        copy.start()

    blocks = lax.broadcasted_iota(jnp.int32, (4, LANES), 0) * LANES
    spots = blocks + lax.broadcasted_iota(jnp.int32, (4, LANES), 1)
    for back in range(SPAN):
        width = width_ref[az(-back)]
        places = spots + (4 * back * LANES - offset_ref[az(-back)])
        inside = (places >= 0) & (places < width)
        places = jnp.where(inside, places, 0).astype(jnp.float32)
        span = jnp.full((4, LANES), width, jnp.int32).astype(jnp.float32)
        taper = 0.5 - 0.5 * jnp.cos((places + 0.5) * (2.0 * math.pi) / span)
        taper_ref[4 * back : 4 * back + 4, :] = jnp.where(inside, taper, 0.0) / jnp.sqrt(span)

    taps_count = 2 * REACH + 1
    distance = jnp.abs(lax.broadcasted_iota(jnp.int32, (2, 4 * LANES), 1) - REACH)
    padded[...] = jnp.zeros_like(padded)
    for wave in range(waves):
        padded[wave, :, :taps_count] = taps_ref[wave]
        rows_of = jnp.where(distance <= reach_ref[wave], padded[wave], 0.0)
        padded[wave] = rows_of
        real = forward_toeplitz(rows_of[0:1])
        imag = forward_toeplitz(rows_of[1:2])
        front[wave, :LANES] = jnp.concatenate([real, -imag], axis=1).astype(jnp.bfloat16)
        front[wave, LANES:] = jnp.concatenate([imag, real], axis=1).astype(jnp.bfloat16)

    loads[1].wait()
    for copy in halo_copies:
        copy.wait_recv()

    def taper(back, block):
        return taper_ref[back * 4 + block : back * 4 + block + 1, :]

    def relay_copy(wave):
        return remote(send_u.at[wave, 3], relay.at[wave], sem_us.at[wave, 3], sem_ur.at[wave, 3], (az(-1), r))

    def spread_u(wave, back):
        for d in range(ht_size):
            if back or d:
                q = ht(d)
                remote(
                    send_u.at[wave, back, q], recv_u.at[wave, back, r],
                    sem_us.at[wave, back], sem_ur.at[wave, back], (az(-back), q),
                ).start()

    def stage_a(wave, carry):
        lhs = windows(x_ref[wave], halo[1, wave], halo[0, wave])
        y = lax.dot_general(lhs, front[wave], ROWS_BY_ROWS, preferred_element_type=jnp.float32)
        stack = []
        for back in range(SPAN):
            row = []
            for part in range(2):
                lanes = slice(part * LANES, (part + 1) * LANES)
                for half in range(2):
                    near = y[half * rows : (half + 1) * rows, lanes] * taper(back, half)
                    far = y[(half + 2) * rows : (half + 3) * rows, lanes] * taper(back, half + 2)
                    row.append((near + far).astype(jnp.bfloat16))
            stack.append(jnp.concatenate(row, axis=1))
        folded = jnp.concatenate(stack, axis=0)
        u = jnp.dot(folded, dft_ref[...], preferred_element_type=jnp.float32).astype(jnp.bfloat16)
        for back in range(SPAN):
            for q in range(ht_size):
                send_u[wave, back, q] = u[back * rows : (back + 1) * rows, q * LANES : (q + 1) * LANES]
        relay_copy(wave).start()
        spread_u(wave, 1)
        spread_u(wave, 0)
        recv_u[wave, 0, r] = send_u[wave, 0, r]
        return carry

    def stage_r(wave, carry):
        relay_copy(wave).wait_recv()
        both = send_u[wave, 2].astype(jnp.float32) + relay[wave].astype(jnp.float32)
        send_u[wave, 2] = both.astype(jnp.bfloat16)
        spread_u(wave, 2)
        return carry

    def await_bytes(ref, sem):
        pltpu.make_async_copy(ref, ref, sem).wait()

    def group(ref, wave, back):
        first = 1 if back == 0 else 0
        return ref.at[wave, back, pl.ds(0, ht_size - first)]

    lane = lax.broadcasted_iota(jnp.int32, (height, LANES), 1)
    sign = jnp.where(lane < LANES // 2, -1.0, 1.0).astype(jnp.float32)

    def stage_b(wave, carry):
        for back in range(3):
            await_bytes(group(recv_u, wave, back), sem_ur.at[wave, back])
        total = recv_u[wave, 0].astype(jnp.float32)
        for back in range(1, 3):
            total = total + recv_u[wave, back].astype(jnp.float32)
        u = total.reshape(height, LANES).astype(jnp.bfloat16)
        z = jnp.dot(prop_ref[wave], u, preferred_element_type=jnp.float32)
        v = z[:height] + sign * pltpu.roll(z[height:], LANES // 2, 1)
        squares = v * v
        power = squares + pltpu.roll(squares, LANES // 2, 1)
        misfit = power - recv_t[:, wave].reshape(height, LANES)
        slope = (2.0 * misfit * v).astype(jnp.bfloat16)
        z = jnp.dot(propt_ref[wave], slope, preferred_element_type=jnp.float32)
        g = z[:height] - sign * pltpu.roll(z[height:], LANES // 2, 1)
        send_g[wave] = g.astype(jnp.bfloat16).reshape(ht_size, rows, LANES)
        for back in (2, 1, 0):
            for d in range(ht_size):
                if back or d:
                    q = ht(d)
                    remote(
                        send_g.at[wave, q], recv_g.at[wave, back, r],
                        sem_gs.at[wave, back], sem_gr.at[wave, back], (az(back), q),
                    ).start()
        recv_g[wave, 0, r] = send_g[wave, r]
        return carry

    def pass_copy(wave):
        return remote(
            recv_g.at[wave, 2], recv_g.at[wave, 3], sem_rs.at[wave], sem_rr.at[wave], (az(1), r)
        )

    def stage_x(wave, carry):
        await_bytes(group(recv_g, wave, 2), sem_gr.at[wave, 2])
        pass_copy(wave).start()
        return carry

    def edge_copy(wave, side):
        return remote(
            gedges.at[wave, side], ghalo.at[wave, side], sem_bs.at[wave, side], sem_br.at[wave, side],
            (az(2 * side - 1), r),
        )

    def stage_c(wave, carry):
        for back in range(2):
            await_bytes(group(recv_g, wave, back), sem_gr.at[wave, back])
        pass_copy(wave).wait_recv()
        stack = []
        for back in range(SPAN):
            stack.append(jnp.concatenate([recv_g[wave, back, q] for q in range(ht_size)], axis=1))
        lhs = jnp.concatenate(stack, axis=0)
        b = lax.dot_general(lhs, dft_ref[...], ROWS_BY_ROWS, preferred_element_type=jnp.float32)
        for part in range(2):
            for block in range(4):
                start = (part * 2 + block % 2) * LANES
                total = b[:rows, start : start + LANES] * taper(0, block)
                for back in range(1, SPAN):
                    piece = b[back * rows : (back + 1) * rows, start : start + LANES]
                    total = total + piece * taper(back, block)
                total = total.astype(jnp.bfloat16)
                place = (part * 4 + block) * LANES
                grad[wave, :, place : place + LANES] = total
                if block in (0, 3):
                    lanes = slice(part * LANES, (part + 1) * LANES)
                    gedges[wave, block // 3, :, lanes] = total
        for side in range(2):
            edge_copy(wave, side).start()
        return carry

    def stage_d(wave, carry):
        for side in range(2):
            edge_copy(wave, side).wait()
        lhs = windows(grad[wave], ghalo[wave, 1], ghalo[wave, 0])
        y = jnp.dot(lhs, behind[wave], preferred_element_type=jnp.float32)
        for block in range(4):
            for part in range(2):
                place = (part * 4 + block) * LANES
                out_ref[wave, :, place : place + LANES] = y[
                    block * rows : (block + 1) * rows, part * LANES : (part + 1) * LANES
                ]
        for back in range(SPAN):
            first = 1 if back == 0 else 0
            await_bytes(group(send_u, wave, back), sem_us.at[wave, back])
            if back < 3:
                await_bytes(send_g.at[wave, pl.ds(0, ht_size - first)], sem_gs.at[wave, back])
        pass_copy(wave).wait_send()
        return carry

    def ahead(wave, carry):
        stage_a(wave, 0)
        lax.cond(wave > 0, lambda: stage_r(wave - 1, 0), lambda: 0)
        return carry

    def middle(step, carry):
        lax.cond(step < waves, lambda: stage_b(step, 0), lambda: 0)
        lax.cond((step > 0) & (step <= waves), lambda: stage_x(step - 1, 0), lambda: 0)
        lax.cond((step > 1) & (step <= waves + 1), lambda: stage_c(step - 2, 0), lambda: 0)
        lax.cond(step > 2, lambda: stage_d(step - 3, 0), lambda: 0)
        return carry

    lax.fori_loop(0, waves, ahead, 0)
    stage_r(waves - 1, 0)
    for wave in range(waves):
        real = backward_toeplitz(padded[wave, 0:1, :])
        imag = backward_toeplitz(padded[wave, 1:2, :])
        behind[wave, : 3 * LANES] = jnp.concatenate([real, -imag], axis=1).astype(jnp.bfloat16)
        behind[wave, 3 * LANES :] = jnp.concatenate([imag, real], axis=1).astype(jnp.bfloat16)
    for load in loads[2:]:
        load.wait()
    for copy in target_copies:
        copy.wait()
    lax.fori_loop(0, waves + 3, middle, 0)
    for copy in halo_copies:
        copy.wait_send()


def on_device(
    object_field, propagator, kernel_taps, band_reach, sector_offset, sector_width, target_index, target_maps,
    *, az_size, ht_size,
):
    rows, waves, parts, length = object_field.shape
    height = propagator.shape[2]
    x = object_field.transpose(1, 0, 2, 3).reshape(waves, rows, parts * length)
    dft = jnp.asarray(dft_table(ht_size))
    prop = propagator.reshape(waves, 2 * height, height)
    propt = propagator.transpose(0, 1, 3, 2).reshape(waves, 2 * height, height)
    maps = target_maps.transpose(0, 2, 1, 3)

    bf16, f32 = jnp.bfloat16, jnp.float32
    dma = pltpu.SemaphoreType.DMA
    vmem = pl.BlockSpec(memory_space=pltpu.VMEM)
    smem = pl.BlockSpec(memory_space=pltpu.SMEM)
    hbm = pl.BlockSpec(memory_space=pltpu.HBM)
    out = pl.pallas_call(
        functools.partial(fused_kernel, az_size, ht_size),
        out_shape=jax.ShapeDtypeStruct((waves, rows, parts * length), f32),
        in_specs=[hbm, vmem, smem, smem, smem, hbm, hbm, hbm, smem, vmem],
        out_specs=vmem,
        scratch_shapes=[
            pltpu.VMEM((ht_size, waves, rows, LANES), f32),
            pltpu.VMEM(x.shape, bf16),
            pltpu.VMEM(dft.shape, bf16),
            pltpu.VMEM(prop.shape, bf16),
            pltpu.VMEM(propt.shape, bf16),
            pltpu.VMEM((4 * SPAN, LANES), f32),
            pltpu.VMEM((waves, 2, 4 * LANES), f32),
            pltpu.VMEM((waves, 2 * LANES, 6 * LANES), bf16),
            pltpu.VMEM((waves, 6 * LANES, 2 * LANES), bf16),
            pltpu.VMEM((waves, ht_size, rows, LANES), bf16),
            pltpu.VMEM((2, waves, rows, 2 * LANES), bf16),
            pltpu.VMEM((2, waves, rows, 2 * LANES), bf16),
            pltpu.VMEM((waves, SPAN, ht_size, rows, LANES), bf16),
            pltpu.VMEM((waves, SPAN, ht_size, rows, LANES), bf16),
            pltpu.VMEM((ht_size, waves, rows, LANES), f32),
            pltpu.VMEM((waves, ht_size, rows, LANES), bf16),
            pltpu.VMEM((waves, SPAN, ht_size, rows, LANES), bf16),
            pltpu.VMEM((waves, rows, parts * length), bf16),
            pltpu.VMEM((waves, 2, rows, 2 * LANES), bf16),
            pltpu.VMEM((waves, 2, rows, 2 * LANES), bf16),
            dma((2,)), dma((2,)),
            dma((waves, SPAN)), dma((waves, SPAN)),
            dma((ht_size,)), dma((ht_size,)),
            dma((waves, SPAN)), dma((waves, SPAN)),
            dma((waves, 2)), dma((waves, 2)), dma((waves,)), dma((waves,)), dma((4,)),
        ],
        compiler_params=pltpu.CompilerParams(
            collective_id=0, has_side_effects=True, vmem_limit_bytes=60 * 1024 * 1024
        ),
    )(x, kernel_taps, band_reach, sector_offset, sector_width, dft, prop, propt, target_index, maps)
    return out.reshape(waves, rows, parts, length).transpose(1, 0, 2, 3)


def solution(mesh):
    in_specs = (P("ht", None, None, "az"), P(), P(), P(), P(), P(), P(), P(None, "ht", None, None))
    out_specs = P("ht", None, None, "az")
    body = functools.partial(on_device, az_size=mesh.shape["az"], ht_size=mesh.shape["ht"])
    return jax.shard_map(body, mesh=mesh, in_specs=in_specs, out_specs=out_specs, check_vma=False)
```
